512 devices in a mesh: seq: 64 (over x, z, core), fsdp: 8 (over y).
Axes of the slice: x: 4, y: 8, z: 8, core: 2. Of those that a mesh axis runs over, the one named last changes fastest.
Arguments:
- query: bfloat16 [8, 8192, 2048], P('fsdp', 'seq'), may hold values from -100 to 100
- key_proj: bfloat16 [8, 8192, 512], P('fsdp', 'seq'), may hold values from -4 to 4
- value_projection_side: bfloat16 [8, 8192, 512], P('fsdp', 'seq'), may hold values from -6 to 6
- residual: bfloat16 [8, 8192, 2048], P('fsdp', 'seq'), may hold values from -6 to 6
- w_out: bfloat16 [2048, 2048], P('fsdp'), may hold values from -0.125 to 0.125
- doc_ids: int32 [8, 8192], P('fsdp'), may hold values from 0 to 31, as said below
- slot_token: int32 [8, 163840], P('fsdp', 'seq'), may hold values from -1 to 8191, as said below
- head_of: int32 [64], replicated, may hold values from 0 to 15, as said below
Outputs:
- layer_out: bfloat16 [8, 8192, 2048], P('fsdp', 'seq')
- slot_stats: float32 [8, 163840], P('fsdp', 'seq')
The draws below stay inside these ranges and needn't reach their ends.
Inputs may be any that keep to these rules, and one draw needn't show every extreme that they name: `doc_ids`: never falling along the pack; each document holds between one half and one and a half times 256 tokens. `slot_token`: the indices of seq form groups of 16 in a row. Each document of a pack belongs to one group, and every device of that group holds all tokens of all documents of its group in its first slots, in increasing order, and -1 in the rest. `head_of`: within each group of 16 indices of seq in a row, every head once.
All inputs are finite; a program needn't handle non-finite values.
Results may differ from the reference program's by a relative error of at most 0.0034.
Values may be sent and summed in bfloat16 or wider, within the bound.
No kernel may reach another device: no remote copies, remote signals or barrier semaphores. Data moves between devices by JAX's collectives and lax.ppermute only.
A program may use at most 64 MiB of HBM per device.

```python
import math
import jax
import jax.numpy as jnp
from jax import lax

QUERY_HEADS = 16
KEY_VALUE_HEADS = 4
HEAD_SIZE = 128
DOUT = 2048
DOC_MEAN = 256
PACK_COUNT = 8
PACK_TOKENS = 8192
DOCS = 32
CAP = 2560
N_SEQ = 64


def pack_layout(pack_key):
    length_key, order_key = jax.random.split(pack_key)
    half_mean = DOC_MEAN // 2
    delta = jax.random.randint(length_key, (DOCS // 2,), -half_mean, half_mean + 1).astype(jnp.int32)
    lengths = jnp.concatenate([DOC_MEAN + delta, DOC_MEAN - delta])
    lengths = jnp.take(lengths, jax.random.permutation(order_key, DOCS)).astype(jnp.int32)
    doc_ends = jnp.cumsum(lengths).astype(jnp.int32)
    places = jnp.arange(PACK_TOKENS, dtype=jnp.int32)
    documents = jnp.sum((places[:, None] >= doc_ends[None, :]).astype(jnp.int32), axis=1)
    group_count = N_SEQ // QUERY_HEADS

    def assign(group_loads, length):
        target = jnp.argmin(group_loads).astype(jnp.int32)
        return (group_loads.at[target].add(length), target)
    group_loads, owners = lax.scan(assign, jnp.zeros((group_count,), jnp.int32), lengths)
    token_group = jnp.take(owners, documents)
    sorted_tokens = jnp.argsort(token_group * PACK_TOKENS + places).astype(jnp.int32)
    offsets = (jnp.cumsum(group_loads) - group_loads).astype(jnp.int32)
    slot_pos = jnp.arange(CAP, dtype=jnp.int32)
    positions = jnp.clip(offsets[:, None] + slot_pos[None, :], 0, PACK_TOKENS - 1)
    group_table = jnp.where(slot_pos[None, :] < group_loads[:, None], jnp.take(sorted_tokens, positions), -1)
    device_table = jnp.repeat(group_table, QUERY_HEADS, axis=0).reshape(-1)
    return (documents, device_table.astype(jnp.int32))


def shared_layout(base_key):
    pack_keys = jax.vmap(lambda number: jax.random.fold_in(base_key, number))(jnp.arange(PACK_COUNT))
    return jax.vmap(pack_layout)(pack_keys)


def drawn_pair(base_key):
    query_key, key_random_seed = jax.random.split(base_key, 2)
    sampled_keys = jnp.clip(jax.random.normal(key_random_seed, (PACK_COUNT, PACK_TOKENS, KEY_VALUE_HEADS, HEAD_SIZE), jnp.float32), -4.0, 4.0)
    sampled_query = jax.random.normal(query_key, (PACK_COUNT, PACK_TOKENS, QUERY_HEADS, HEAD_SIZE), jnp.float32)
    return (sampled_query.reshape(PACK_COUNT, PACK_TOKENS, QUERY_HEADS * HEAD_SIZE), sampled_keys.reshape(PACK_COUNT, PACK_TOKENS, KEY_VALUE_HEADS * HEAD_SIZE))


def draw_query(key, part):
    return drawn_pair(key)[0].astype(jnp.bfloat16)


def draw_key_proj(key, part):
    return drawn_pair(key)[1].astype(jnp.bfloat16)


def draw_doc_ids(key, part):
    return shared_layout(key)[0].astype(jnp.int32)


def draw_slot_token(key, part):
    return shared_layout(key)[1].astype(jnp.int32)


def draw_head_of(key, part):
    key = jax.random.fold_in(key, 11)
    group_keys = jax.random.split(key, N_SEQ // QUERY_HEADS)
    orders = jax.vmap(lambda group_key: jax.random.permutation(group_key, QUERY_HEADS))(group_keys)
    return orders.reshape(-1).astype(jnp.int32)


def block_scale(key, extent, shards, least, top_value):
    gain, own = 1.0, jax.random.fold_in(key, 6)
    for axis_at, parts in shards:
        draws = jnp.exp(jax.random.uniform(jax.random.fold_in(own, axis_at), (parts,), jnp.float32, least / len(shards), top_value / len(shards)))
        gain = gain * jnp.repeat(draws, extent[axis_at] // parts).reshape([-1 if axis == axis_at else 1 for axis in range(len(extent))])
    return gain


def normal_values(key, extent, width, bound, shards=(), held_as=jnp.bfloat16):
    entries = jax.random.normal(key, extent, jnp.float32) * width
    if len(shards) > 0:
        entries = block_scale(key, extent, shards, -0.22, 0.18) * entries
    return jnp.clip(entries, min=-bound, max=bound).astype(held_as)


def setup_inputs(seed: int = 0) -> dict:
    key_list = jax.random.split(jax.random.key(seed), 9)
    query = draw_query(jax.random.fold_in(key_list[8], 71), 0)
    key_proj = draw_key_proj(jax.random.fold_in(key_list[8], 71), 0)
    value_projection_side = normal_values(key_list[2], (PACK_COUNT, PACK_TOKENS, KEY_VALUE_HEADS * HEAD_SIZE), 1.0, 6.0, ((0, 8), (1, 64)))
    residual = normal_values(key_list[3], (PACK_COUNT, PACK_TOKENS, DOUT), 1.0, 6.0, ((0, 8), (1, 64)))
    w_out = normal_values(key_list[4], (QUERY_HEADS * HEAD_SIZE, DOUT), (QUERY_HEADS * HEAD_SIZE) ** -0.5, 0.125, ((0, 8),))
    doc_ids = draw_doc_ids(jax.random.fold_in(key_list[8], 71), 0)
    slot_token = draw_slot_token(jax.random.fold_in(key_list[8], 71), 0)
    head_of = draw_head_of(jax.random.fold_in(key_list[8], 71), 0)
    return dict(query=query, key_proj=key_proj, value_projection_side=value_projection_side, residual=residual, w_out=w_out, doc_ids=doc_ids, slot_token=slot_token, head_of=head_of)


def attend(query_rows, key_row_block, value_row_block, documents):
    row_count_total = query_rows.shape[0]
    block = math.gcd(row_count_total, 128)
    window = min(row_count_total, block + 2 * DOC_MEAN)
    query_per_key_group = QUERY_HEADS // KEY_VALUE_HEADS
    score_scale = 1.0 / math.sqrt(HEAD_SIZE)
    query_heads = query_rows.reshape(row_count_total, QUERY_HEADS, HEAD_SIZE)
    key_head_split = jnp.repeat(key_row_block.reshape(row_count_total, KEY_VALUE_HEADS, HEAD_SIZE), query_per_key_group, axis=1)
    value_head_split = jnp.repeat(value_row_block.reshape(row_count_total, KEY_VALUE_HEADS, HEAD_SIZE), query_per_key_group, axis=1)

    def one_block(begin_row):
        key_start = jnp.clip(begin_row + block - window, 0, row_count_total - window).astype(jnp.int32)
        query_block = lax.dynamic_slice_in_dim(query_heads, begin_row, block, 0).astype(jnp.float32)
        key_block = lax.dynamic_slice_in_dim(key_head_split, key_start, window, 0).astype(jnp.float32)
        value_block = lax.dynamic_slice_in_dim(value_head_split, key_start, window, 0).astype(jnp.float32)
        scores = jnp.einsum('ihd,jhd->hij', query_block, key_block) * score_scale
        query_docs = lax.dynamic_slice_in_dim(documents, begin_row, block, 0)
        key_docs = lax.dynamic_slice_in_dim(documents, key_start, window, 0)
        query_pos = begin_row + jnp.arange(block, dtype=jnp.int32)
        key_pos = key_start + jnp.arange(window, dtype=jnp.int32)
        allowed = (query_docs[:, None] == key_docs[None, :]) & (key_pos[None, :] <= query_pos[:, None])
        scores = jnp.where(allowed[None], scores, -jnp.inf)
        top = lax.optimization_barrier(jnp.max(scores, axis=2, keepdims=True))
        weights = jnp.exp(scores - top)
        totals = lax.optimization_barrier(jnp.sum(weights, axis=2, keepdims=True))
        share = lax.optimization_barrier((weights / totals).astype(jnp.bfloat16)).astype(jnp.float32)
        mixed = jnp.einsum('hij,jhd->ihd', share, value_block).astype(jnp.bfloat16)
        log_total = (top + jnp.log(totals))[:, :, 0].T
        return (mixed, log_total)
    starts = jnp.arange(row_count_total // block, dtype=jnp.int32) * block
    mixed, log_total = lax.map(one_block, starts)
    return (mixed.reshape(row_count_total, QUERY_HEADS * HEAD_SIZE), log_total.reshape(row_count_total, QUERY_HEADS))

def reference(query, key_proj, value_projection_side, residual, w_out, doc_ids, slot_token, head_of):

    def per_pack(items):
        query_rows, key_row_block, value_row_block, residual_rows, documents = items
        mixed, log_total = attend(query_rows, key_row_block, value_row_block, documents)
        projected = jnp.dot(mixed, w_out, preferred_element_type=jnp.float32)
        layer_rows = (residual_rows.astype(jnp.float32) + projected).astype(jnp.bfloat16)
        return (layer_rows, log_total)
    layer_out, log_totals = lax.map(per_pack, (query, key_proj, value_projection_side, residual, doc_ids))
    slot_heads = jnp.repeat(head_of, CAP)
    safe_tokens = jnp.maximum(slot_token, 0)
    pack_index = jnp.arange(PACK_COUNT, dtype=jnp.int32)[:, None]
    picked = log_totals[pack_index, safe_tokens, slot_heads[None, :]]
    slot_stats = jnp.where(slot_token >= 0, picked, jnp.float32(0.0))
    return (layer_out, slot_stats)
```

```python
import functools
import math

import jax
import jax.numpy as jnp
from jax import lax
from jax.experimental import pallas as pl
from jax.experimental.pallas import tpu as pltpu
from jax.sharding import Mesh, PartitionSpec as P

HEAD_SIZE = 128
BLOCK = 128
BACK = 3
SCALE = 1.0 / math.sqrt(HEAD_SIZE)
SEQ = ("x", "z", "core")
VMEM = pltpu.CompilerParams(vmem_limit_bytes=48 * 1024 * 1024)


def attend_kernel(heads, kv_heads, head_of_ref, q_ref, bias_ref, kv3_ref, kv2_ref, kv1_ref, kv0_ref, mixed_ref, send_ref, lt_ref):
    per = heads // kv_heads
    width = kv_heads * HEAD_SIZE
    pieces = (kv3_ref, kv2_ref, kv1_ref, kv0_ref)
    bias = bias_ref[...]
    for g in range(kv_heads):
        at = g * HEAD_SIZE
        k = jnp.concatenate([p[:, at : at + HEAD_SIZE] for p in pieces], axis=0)
        v = jnp.concatenate([p[:, width + at : width + at + HEAD_SIZE] for p in pieces], axis=0)
        for h in range(g * per, (g + 1) * per):
            cols = slice(h * HEAD_SIZE, (h + 1) * HEAD_SIZE)
            s = lax.dot_general(k, q_ref[:, cols], (((1,), (1,)), ((), ())), preferred_element_type=jnp.float32)
            s = s + bias
            top = jnp.max(s, axis=0, keepdims=True)
            w = jnp.exp2((s - top) * (SCALE * math.log2(math.e)))
            total = jnp.sum(w, axis=0, keepdims=True)
            share = (w * (1.0 / total)).astype(jnp.bfloat16)
            mixed = lax.dot_general(v, share, (((0,), (0,)), ((), ())), preferred_element_type=jnp.float32)
            mixed_ref[:, cols] = mixed.T.astype(jnp.bfloat16)
            lt_ref[h : h + 1, :] = top * SCALE + jnp.log(total)
    for d in range(send_ref.shape[0]):
        send_ref[d : d + 1, :] = lt_ref[pl.ds(head_of_ref[d], 1), :]


def slots_kernel(got_ref, slot_ref, out_ref):
    slots = slot_ref[...]
    row = slots >> 7
    lane = slots & 127
    out = jnp.zeros(slots.shape, jnp.float32)
    for r in range(got_ref.shape[0]):
        source = jnp.broadcast_to(got_ref[r : r + 1, :], slots.shape)
        out = jnp.where(row == r, jnp.take_along_axis(source, lane, axis=1), out)
    out_ref[...] = out


def local(query, key_proj, value_projection_side, residual, w_out, doc_ids, slot_token, head_of):
    tok_rows = query.shape[1]
    heads = query.shape[2] // HEAD_SIZE
    kv_heads = key_proj.shape[2] // HEAD_SIZE
    seq_count = lax.axis_size(SEQ)
    me = lax.axis_index(SEQ)
    cores = lax.axis_size("core")
    part = w_out.shape[0] // cores
    w_part = lax.dynamic_slice_in_dim(w_out, lax.axis_index("core") * part, part, 0)
    w_all = lax.all_gather(w_part, ("fsdp", "core"), axis=0, tiled=True)

    kv = jnp.concatenate([key_proj[0], value_projection_side[0]], axis=1)
    before = [
        lax.ppermute(kv, SEQ, [(i, (i + back) % seq_count) for i in range(seq_count)])
        for back in range(1, BACK + 1)
    ]
    back_rows = BACK * tok_rows
    window = back_rows + tok_rows
    padded = jnp.concatenate([jnp.full((back_rows,), -1, jnp.int32), doc_ids[0]])
    docs = lax.dynamic_slice_in_dim(padded, me * tok_rows, window, 0)
    key_at = jnp.arange(window, dtype=jnp.int32)
    query_at = back_rows + jnp.arange(tok_rows, dtype=jnp.int32)
    allowed = (docs[:, None] == docs[None, back_rows:]) & (key_at[:, None] <= query_at[None, :])
    bias = jnp.where(allowed, 0.0, -1e30).astype(jnp.float32)

    whole = pl.BlockSpec(memory_space=pltpu.VMEM)
    mixed, send = pl.pallas_call(
        functools.partial(attend_kernel, heads, kv_heads),
        out_shape=(
            jax.ShapeDtypeStruct((tok_rows, heads * HEAD_SIZE), jnp.bfloat16),
            jax.ShapeDtypeStruct((seq_count, tok_rows), jnp.float32),
        ),
        in_specs=[pl.BlockSpec(memory_space=pltpu.SMEM)] + [whole] * 6,
        out_specs=(whole, whole),
        scratch_shapes=[pltpu.VMEM((heads, tok_rows), jnp.float32)],
        compiler_params=VMEM,
    )(head_of, query[0], bias, before[2], before[1], before[0], kv)

    got = lax.all_to_all(send, SEQ, split_axis=0, concat_axis=0, tiled=True)
    capacity = slot_token.shape[1]
    stats = pl.pallas_call(
        slots_kernel,
        out_shape=jax.ShapeDtypeStruct((capacity // 128, 128), jnp.float32),
        in_specs=[whole, whole],
        out_specs=whole,
        compiler_params=VMEM,
    )(got, slot_token.reshape(capacity // 128, 128))

    projected = jnp.dot(mixed, w_all, preferred_element_type=jnp.float32)
    layer_out = (residual[0].astype(jnp.float32) + projected).astype(jnp.bfloat16)[None]
    return (layer_out, stats.reshape(1, capacity))


def solution(mesh):
    split = Mesh(mesh.devices.reshape(4, 8, 2, 8), ("x", "z", "core", "fsdp"))
    return jax.shard_map(
        local,
        mesh=split,
        in_specs=(
            P("fsdp", SEQ, None),
            P("fsdp", SEQ, None),
            P("fsdp", SEQ, None),
            P("fsdp", SEQ, None),
            P("fsdp", None),
            P("fsdp", None),
            P("fsdp", SEQ),
            P(),
        ),
        out_specs=(P("fsdp", SEQ, None), P("fsdp", SEQ)),
        check_vma=False,
    )
```

```python
import functools
import math

import jax
import jax.numpy as jnp
from jax import lax
from jax.experimental import pallas as pl
from jax.experimental.pallas import tpu as pltpu
from jax.sharding import Mesh, PartitionSpec as P

HEAD_SIZE = 128
BLOCK = 128
BACK = 3
SCALE = 1.0 / math.sqrt(HEAD_SIZE)
SEQ = ("x", "z", "core")
VMEM = pltpu.CompilerParams(vmem_limit_bytes=14 * 1024 * 1024)
STREAM = pltpu.CompilerParams(vmem_limit_bytes=56 * 1024 * 1024)


def attend_kernel(heads, kv_heads, head_of_ref, q_ref, bias_ref, kv0_ref, kv1_ref, kv2_ref, kv3_ref, mixed_ref, send_ref, lt_ref):
    per = heads // kv_heads
    width = kv_heads * HEAD_SIZE
    pieces = (kv0_ref, kv1_ref, kv2_ref, kv3_ref)
    bias = bias_ref[...]
    for g in range(kv_heads):
        at = g * HEAD_SIZE
        k = jnp.concatenate([p[:, at : at + HEAD_SIZE] for p in pieces], axis=0)
        v = jnp.concatenate([p[:, width + at : width + at + HEAD_SIZE] for p in pieces], axis=0)
        for h in range(g * per, (g + 1) * per):
            cols = slice(h * HEAD_SIZE, (h + 1) * HEAD_SIZE)
            s = lax.dot_general(k, q_ref[:, cols], (((1,), (1,)), ((), ())), preferred_element_type=jnp.float32)
            s = s + bias
            top = jnp.max(s, axis=0, keepdims=True)
            w = jnp.exp2((s - top) * (SCALE * math.log2(math.e)))
            total = jnp.sum(w, axis=0, keepdims=True)
            share = (w * (1.0 / total)).astype(jnp.bfloat16)
            mixed = lax.dot_general(v, share, (((0,), (0,)), ((), ())), preferred_element_type=jnp.float32)
            mixed_ref[:, cols] = mixed.T.astype(jnp.bfloat16)
            lt_ref[h : h + 1, :] = top * SCALE + jnp.log(total)
    for d in range(send_ref.shape[0]):
        send_ref[d : d + 1, :] = lt_ref[pl.ds(head_of_ref[d], 1), :]


def slots_kernel(got_ref, slot_ref, out_ref):
    slots = slot_ref[...]
    row = slots >> 7
    lane = slots & 127
    out = jnp.zeros(slots.shape, jnp.float32)
    for r in range(got_ref.shape[0]):
        source = jnp.broadcast_to(got_ref[r : r + 1, :], slots.shape)
        out = jnp.where(row == r, jnp.take_along_axis(source, lane, axis=1), out)
    out_ref[...] = out


def streamed(tokens_ref, weight_ref, held_ref, rows_ref, sems):
    count = sems.shape[0] - 1
    step = weight_ref.shape[0] // count
    parts = [pl.ds(i * step, step) for i in range(count)]
    tokens = pltpu.make_async_copy(tokens_ref, rows_ref, sems.at[count])
    copies = [pltpu.make_async_copy(weight_ref.at[p], held_ref.at[p], sems.at[i]) for i, p in enumerate(parts)]
    tokens.start()
    for copy in copies:
        copy.start()
    tokens.wait()
    total = None
    for copy, part in zip(copies, parts):
        copy.wait()
        product = jnp.dot(rows_ref[:, part], held_ref[part, :], preferred_element_type=jnp.float32)
        total = product if total is None else total + product
    return total


def away_kernel(tokens_ref, weight_ref, out_ref, held_ref, rows_ref, sems):
    out_ref[...] = streamed(tokens_ref, weight_ref, held_ref, rows_ref, sems).astype(jnp.bfloat16)


def here_kernel(side_ref, tokens_ref, weight_ref, residual_ref, out_ref, held_ref, rows_ref, sems, half_ref, sem):
    width = half_ref.shape[1]
    mine = pl.ds(pl.multiple_of(side_ref[0] * width, width), width)
    total = streamed(tokens_ref, weight_ref, held_ref, rows_ref, sems)
    half_ref[...] = (residual_ref[:, mine].astype(jnp.float32) + total).astype(jnp.bfloat16)
    copy = pltpu.make_async_copy(half_ref, out_ref.at[:, mine], sem)
    copy.start()
    copy.wait()


def join_kernel(side_ref, here_ref, back_ref, residual_ref, out_ref, half_ref, sem):
    width = half_ref.shape[1]
    theirs = pl.ds(pl.multiple_of((1 - side_ref[0]) * width, width), width)
    total = residual_ref[:, theirs].astype(jnp.float32) + back_ref[...].astype(jnp.float32)
    half_ref[...] = total.astype(jnp.bfloat16)
    copy = pltpu.make_async_copy(half_ref, out_ref.at[:, theirs], sem)
    copy.start()
    copy.wait()


def after(x, *others):
    anywhere = pl.BlockSpec(memory_space=pl.ANY)
    return pl.pallas_call(
        lambda *refs: None,
        out_shape=jax.ShapeDtypeStruct(x.shape, x.dtype),
        in_specs=[anywhere] * (1 + len(others)),
        out_specs=anywhere,
        input_output_aliases={0: 0},
        compiler_params=pltpu.CompilerParams(vmem_limit_bytes=1024 * 1024),
    )(x, *others)


def local(query, key_proj, value_projection_side, residual, w_out, doc_ids, slot_token, head_of):
    tok_rows = query.shape[1]
    heads = query.shape[2] // HEAD_SIZE
    kv_heads = key_proj.shape[2] // HEAD_SIZE
    seq_count = lax.axis_size(SEQ)
    me = lax.axis_index(SEQ)
    core = lax.axis_index("core")
    side = lax.axis_index("x") % 2
    half = w_out.shape[0] // 2
    columns = w_out.shape[1]
    width = columns // 2
    swap = [(i, i ^ 1) for i in range(seq_count)]
    pair = [(i, i ^ 1) for i in range(lax.axis_size("x"))]

    anywhere = pl.BlockSpec(memory_space=pl.ANY)
    whole = pl.BlockSpec(memory_space=pltpu.VMEM)
    scalars = pl.BlockSpec(memory_space=pltpu.SMEM)
    part = lax.dynamic_slice(w_out, (core * half, side * width), (half, width))
    weight = lax.all_gather(part, ("fsdp", "core"), axis=0, tiled=True)

    kv = jnp.concatenate([key_proj[0], value_projection_side[0]], axis=1)
    kv1 = lax.ppermute(kv, SEQ, [(i, (i + 2) % seq_count) for i in range(seq_count)])
    kv2 = lax.ppermute(kv, SEQ, [(i, (i + (3 if i % 2 else 1)) % seq_count) for i in range(seq_count)])
    kv3 = lax.ppermute(kv1, SEQ, swap)

    back_rows = BACK * tok_rows
    padded = jnp.concatenate([jnp.full((back_rows,), -1, jnp.int32), doc_ids[0]])
    behind = (0, 2, 3 - 2 * core, 1 + 2 * core)
    query_docs = lax.dynamic_slice_in_dim(padded, (me + BACK) * tok_rows, tok_rows, 0)
    docs = jnp.concatenate([lax.dynamic_slice_in_dim(padded, (me + BACK - b) * tok_rows, tok_rows, 0) for b in behind])
    key_at = jnp.arange((BACK + 1) * tok_rows, dtype=jnp.int32)
    query_at = jnp.arange(tok_rows, dtype=jnp.int32)
    allowed = (docs[:, None] == query_docs[None, :]) & (
        (key_at[:, None] >= tok_rows) | (key_at[:, None] <= query_at[None, :])
    )
    bias = jnp.where(allowed, 0.0, -1e30).astype(jnp.float32)

    mixed, send = pl.pallas_call(
        functools.partial(attend_kernel, heads, kv_heads),
        out_shape=(
            jax.ShapeDtypeStruct((tok_rows, heads * HEAD_SIZE), jnp.bfloat16),
            jax.ShapeDtypeStruct((seq_count, tok_rows), jnp.float32),
        ),
        in_specs=[scalars] + [whole] * 6,
        out_specs=(whole, whole),
        scratch_shapes=[pltpu.VMEM((heads, tok_rows), jnp.float32)],
        compiler_params=VMEM,
    )(head_of, query[0], bias, kv, kv1, kv2, kv3)

    theirs = lax.ppermute(mixed, "x", pair)
    got = lax.all_to_all(send, SEQ, split_axis=0, concat_axis=0, tiled=True)
    capacity = slot_token.shape[1]
    stats = pl.pallas_call(
        slots_kernel,
        out_shape=jax.ShapeDtypeStruct((capacity // 128, 128), jnp.float32),
        in_specs=[whole, whole],
        out_specs=whole,
        compiler_params=VMEM,
    )(got, slot_token.reshape(capacity // 128, 128))
    theirs = after(theirs, got)
    scratch = [
        pltpu.VMEM((columns, width), jnp.bfloat16),
        pltpu.VMEM((tok_rows, columns), jnp.bfloat16),
        pltpu.SemaphoreType.DMA((9,)),
    ]
    half_scratch = [pltpu.VMEM((tok_rows, width), jnp.bfloat16), pltpu.SemaphoreType.DMA]
    away = pl.pallas_call(
        away_kernel,
        out_shape=jax.ShapeDtypeStruct((tok_rows, width), jnp.bfloat16),
        in_specs=[anywhere, anywhere],
        out_specs=whole,
        scratch_shapes=scratch,
        compiler_params=STREAM,
    )(theirs, weight)
    back = lax.ppermute(away, "x", pair)
    result = jax.ShapeDtypeStruct((tok_rows, columns), jnp.bfloat16)
    side = side[None].astype(jnp.int32)
    here = pl.pallas_call(
        here_kernel,
        out_shape=result,
        in_specs=[scalars, anywhere, anywhere, whole],
        out_specs=anywhere,
        scratch_shapes=scratch + half_scratch,
        compiler_params=STREAM,
    )(side, mixed, weight, residual[0])
    layer_out = pl.pallas_call(
        join_kernel,
        out_shape=result,
        in_specs=[scalars, anywhere, whole, whole],
        out_specs=anywhere,
        scratch_shapes=half_scratch,
        input_output_aliases={1: 0},
        compiler_params=VMEM,
    )(side, here, back, residual[0])
    return (layer_out[None], stats.reshape(1, capacity))


def solution(mesh):
    split = Mesh(mesh.devices.reshape(4, 8, 2, 8), ("x", "z", "core", "fsdp"))
    return jax.shard_map(
        local,
        mesh=split,
        in_specs=(
            P("fsdp", SEQ, None),
            P("fsdp", SEQ, None),
            P("fsdp", SEQ, None),
            P("fsdp", SEQ, None),
            P("fsdp", None),
            P("fsdp", None),
            P("fsdp", SEQ),
            P(),
        ),
        out_specs=(P("fsdp", SEQ, None), P("fsdp", SEQ)),
        check_vma=False,
    )
```

```python
import functools
import math

import jax
import jax.numpy as jnp
from jax import lax
from jax.experimental import pallas as pl
from jax.experimental.pallas import tpu as pltpu
from jax.sharding import Mesh, PartitionSpec as P

HEAD_SIZE = 128
BLOCK = 128
BACK = 3
SCALE = 1.0 / math.sqrt(HEAD_SIZE)
SEQ = ("x", "z", "core")
VMEM = pltpu.CompilerParams(vmem_limit_bytes=14 * 1024 * 1024)
STREAM = pltpu.CompilerParams(vmem_limit_bytes=56 * 1024 * 1024)


def attend_kernel(heads, kv_heads, head_of_ref, q_ref, bias_ref, kv0_ref, kv1_ref, kv2_ref, kv3_ref, mixed_ref, send_ref, lt_ref):
    per = heads // kv_heads
    width = kv_heads * HEAD_SIZE
    pieces = (kv0_ref, kv1_ref, kv2_ref, kv3_ref)
    bias = bias_ref[...]
    for g in range(kv_heads):
        at = g * HEAD_SIZE
        k = jnp.concatenate([p[:, at : at + HEAD_SIZE] for p in pieces], axis=0)
        v = jnp.concatenate([p[:, width + at : width + at + HEAD_SIZE] for p in pieces], axis=0)
        for h in range(g * per, (g + 1) * per):
            cols = slice(h * HEAD_SIZE, (h + 1) * HEAD_SIZE)
            s = lax.dot_general(k, q_ref[:, cols], (((1,), (1,)), ((), ())), preferred_element_type=jnp.float32)
            s = s + bias
            top = jnp.max(s, axis=0, keepdims=True)
            w = jnp.exp2((s - top) * (SCALE * math.log2(math.e)))
            total = jnp.sum(w, axis=0, keepdims=True)
            share = (w * (1.0 / total)).astype(jnp.bfloat16)
            mixed = lax.dot_general(v, share, (((0,), (0,)), ((), ())), preferred_element_type=jnp.float32)
            mixed_ref[:, cols] = mixed.T.astype(jnp.bfloat16)
            lt_ref[h : h + 1, :] = top * SCALE + jnp.log(total)
    for d in range(send_ref.shape[0]):
        send_ref[d : d + 1, :] = lt_ref[pl.ds(head_of_ref[d], 1), :]


def slots_kernel(got_ref, slot_ref, out_ref):
    slots = slot_ref[...]
    row = slots >> 7
    lane = slots & 127
    out = jnp.zeros(slots.shape, jnp.float32)
    for r in range(got_ref.shape[0]):
        source = jnp.broadcast_to(got_ref[r : r + 1, :], slots.shape)
        out = jnp.where(row == r, jnp.take_along_axis(source, lane, axis=1), out)
    for r in range(slots.shape[0]):
        out_ref[:, r * 128 : (r + 1) * 128] = out[r : r + 1, :]


def streamed(tokens_ref, weight_ref, held_ref, rows_ref, sems):
    count = sems.shape[0] - 1
    step = weight_ref.shape[0] // count
    parts = [pl.ds(i * step, step) for i in range(count)]
    tokens = pltpu.make_async_copy(tokens_ref, rows_ref, sems.at[count])
    copies = [pltpu.make_async_copy(weight_ref.at[p], held_ref.at[p], sems.at[i]) for i, p in enumerate(parts)]
    tokens.start()
    for copy in copies:
        copy.start()
    tokens.wait()
    total = None
    for copy, part in zip(copies, parts):
        copy.wait()
        product = jnp.dot(rows_ref[:, part], held_ref[part, :], preferred_element_type=jnp.float32)
        total = product if total is None else total + product
    return total


def away_kernel(tokens_ref, weight_ref, out_ref, held_ref, rows_ref, sems):
    out_ref[...] = streamed(tokens_ref, weight_ref, held_ref, rows_ref, sems).astype(jnp.bfloat16)


def here_kernel(side_ref, tokens_ref, weight_ref, residual_ref, out_ref, held_ref, rows_ref, sems, half_ref, sem):
    width = half_ref.shape[1]
    mine = pl.ds(pl.multiple_of(side_ref[0] * width, width), width)
    total = streamed(tokens_ref, weight_ref, held_ref, rows_ref, sems)
    half_ref[...] = (residual_ref[:, mine].astype(jnp.float32) + total).astype(jnp.bfloat16)
    copy = pltpu.make_async_copy(half_ref, out_ref.at[:, mine], sem)
    copy.start()
    copy.wait()


def join_kernel(side_ref, here_ref, back_ref, residual_ref, out_ref, half_ref, sem):
    width = half_ref.shape[1]
    theirs = pl.ds(pl.multiple_of((1 - side_ref[0]) * width, width), width)
    total = residual_ref[:, theirs].astype(jnp.float32) + back_ref[...].astype(jnp.float32)
    half_ref[...] = total.astype(jnp.bfloat16)
    copy = pltpu.make_async_copy(half_ref, out_ref.at[:, theirs], sem)
    copy.start()
    copy.wait()


def after(x, *others):
    whole = pl.BlockSpec(memory_space=pltpu.VMEM)
    return pl.pallas_call(
        lambda *refs: None,
        out_shape=jax.ShapeDtypeStruct(x.shape, x.dtype),
        in_specs=[whole] * (1 + len(others)),
        out_specs=whole,
        input_output_aliases={0: 0},
        compiler_params=VMEM,
    )(x, *others)


def local(query, key_proj, value_projection_side, residual, w_out, doc_ids, slot_token, head_of):
    tok_rows = query.shape[1]
    heads = query.shape[2] // HEAD_SIZE
    kv_heads = key_proj.shape[2] // HEAD_SIZE
    seq_count = lax.axis_size(SEQ)
    me = lax.axis_index(SEQ)
    core = lax.axis_index("core")
    side = (lax.axis_index("x") + lax.axis_index("z")) % 2
    half = w_out.shape[0] // 2
    columns = w_out.shape[1]
    width = columns // 2
    swap = [(i, i ^ 1) for i in range(seq_count)]
    cores, row = lax.axis_size("core"), lax.axis_size("z") * lax.axis_size("core")
    pair = [(i, (i // row ^ 1) * row + i % row if i % cores == 0 else i ^ cores) for i in range(seq_count)]

    anywhere = pl.BlockSpec(memory_space=pl.ANY)
    whole = pl.BlockSpec(memory_space=pltpu.VMEM)
    scalars = pl.BlockSpec(memory_space=pltpu.SMEM)
    part = lax.dynamic_slice(w_out, (core * half, side * width), (half, width))
    weight = lax.all_gather(part, ("fsdp", "core"), axis=0, tiled=True)

    kv = jnp.concatenate([key_proj[0], value_projection_side[0]], axis=1)
    kv1 = lax.ppermute(kv, SEQ, [(i, (i + 2) % seq_count) for i in range(seq_count)])
    kv2 = lax.ppermute(kv, SEQ, [(i, (i + (3 if i % 2 else 1)) % seq_count) for i in range(seq_count)])
    kv3 = lax.ppermute(kv1, SEQ, swap)

    back_rows = BACK * tok_rows
    padded = jnp.concatenate([jnp.full((back_rows,), -1, jnp.int32), doc_ids[0]])
    behind = (0, 2, 3 - 2 * core, 1 + 2 * core)
    query_docs = lax.dynamic_slice_in_dim(padded, (me + BACK) * tok_rows, tok_rows, 0)
    docs = jnp.concatenate([lax.dynamic_slice_in_dim(padded, (me + BACK - b) * tok_rows, tok_rows, 0) for b in behind])
    key_at = jnp.arange((BACK + 1) * tok_rows, dtype=jnp.int32)
    query_at = jnp.arange(tok_rows, dtype=jnp.int32)
    allowed = (docs[:, None] == query_docs[None, :]) & (
        (key_at[:, None] >= tok_rows) | (key_at[:, None] <= query_at[None, :])
    )
    bias = jnp.where(allowed, 0.0, -1e30).astype(jnp.float32)

    mixed, send = pl.pallas_call(
        functools.partial(attend_kernel, heads, kv_heads),
        out_shape=(
            jax.ShapeDtypeStruct((tok_rows, heads * HEAD_SIZE), jnp.bfloat16),
            jax.ShapeDtypeStruct((seq_count, tok_rows), jnp.float32),
        ),
        in_specs=[scalars] + [whole] * 6,
        out_specs=(whole, whole),
        scratch_shapes=[pltpu.VMEM((heads, tok_rows), jnp.float32)],
        compiler_params=VMEM,
    )(head_of, query[0], bias, kv, kv1, kv2, kv3)

    theirs = lax.ppermute(mixed, SEQ, pair)
    got = lax.all_to_all(send, SEQ, split_axis=0, concat_axis=0, tiled=True)
    capacity = slot_token.shape[1]
    stats = pl.pallas_call(
        slots_kernel,
        out_shape=jax.ShapeDtypeStruct((1, capacity), jnp.float32),
        in_specs=[whole, whole],
        out_specs=whole,
        compiler_params=VMEM,
    )(got, slot_token.reshape(capacity // 128, 128))
    theirs = after(theirs, stats)
    scratch = [
        pltpu.VMEM((columns, width), jnp.bfloat16),
        pltpu.VMEM((tok_rows, columns), jnp.bfloat16),
        pltpu.SemaphoreType.DMA((9,)),
    ]
    half_scratch = [pltpu.VMEM((tok_rows, width), jnp.bfloat16), pltpu.SemaphoreType.DMA]
    away = pl.pallas_call(
        away_kernel,
        out_shape=jax.ShapeDtypeStruct((tok_rows, width), jnp.bfloat16),
        in_specs=[anywhere, anywhere],
        out_specs=whole,
        scratch_shapes=scratch,
        compiler_params=STREAM,
    )(theirs, weight)
    back = lax.ppermute(away, SEQ, pair)
    result = jax.ShapeDtypeStruct((tok_rows, columns), jnp.bfloat16)
    side = side[None].astype(jnp.int32)
    here = pl.pallas_call(
        here_kernel,
        out_shape=result,
        in_specs=[scalars, anywhere, anywhere, whole],
        out_specs=anywhere,
        scratch_shapes=scratch + half_scratch,
        compiler_params=STREAM,
    )(side, mixed, weight, residual[0])
    layer_out = pl.pallas_call(
        join_kernel,
        out_shape=result,
        in_specs=[scalars, anywhere, whole, whole],
        out_specs=anywhere,
        scratch_shapes=half_scratch,
        input_output_aliases={1: 0},
        compiler_params=VMEM,
    )(side, here, back, residual[0])
    return (layer_out[None], stats)


def solution(mesh):
    split = Mesh(mesh.devices.reshape(4, 8, 2, 8), ("x", "z", "core", "fsdp"))
    return jax.shard_map(
        local,
        mesh=split,
        in_specs=(
            P("fsdp", SEQ, None),
            P("fsdp", SEQ, None),
            P("fsdp", SEQ, None),
            P("fsdp", SEQ, None),
            P("fsdp", None),
            P("fsdp", None),
            P("fsdp", SEQ),
            P(),
        ),
        out_specs=(P("fsdp", SEQ, None), P("fsdp", SEQ)),
        check_vma=False,
    )
```

```python
import functools
import math

import jax
import jax.numpy as jnp
from jax import lax
from jax.experimental import pallas as pl
from jax.experimental.pallas import tpu as pltpu
from jax.sharding import Mesh, PartitionSpec as P

HEAD_SIZE = 128
BLOCK = 128
BACK = 3
SCALE = 1.0 / math.sqrt(HEAD_SIZE)
SEQ = ("x", "z", "core")
VMEM = pltpu.CompilerParams(vmem_limit_bytes=14 * 1024 * 1024)
STREAM = pltpu.CompilerParams(vmem_limit_bytes=56 * 1024 * 1024)


def attend_kernel(heads, kv_heads, head_of_ref, q_ref, bias_ref, kv0_ref, kv1_ref, kv2_ref, kv3_ref, mixed_ref, send_ref, lt_ref):
    per = heads // kv_heads
    width = kv_heads * HEAD_SIZE
    pieces = (kv0_ref, kv1_ref, kv2_ref, kv3_ref)
    bias = bias_ref[...]
    for g in range(kv_heads):
        at = g * HEAD_SIZE
        k = jnp.concatenate([p[:, at : at + HEAD_SIZE] for p in pieces], axis=0)
        v = jnp.concatenate([p[:, width + at : width + at + HEAD_SIZE] for p in pieces], axis=0)
        for h in range(g * per, (g + 1) * per):
            cols = slice(h * HEAD_SIZE, (h + 1) * HEAD_SIZE)
            s = lax.dot_general(k, q_ref[:, cols], (((1,), (1,)), ((), ())), preferred_element_type=jnp.float32)
            s = s + bias
            top = jnp.max(s, axis=0, keepdims=True)
            w = jnp.exp2((s - top) * (SCALE * math.log2(math.e)))
            total = jnp.sum(w, axis=0, keepdims=True)
            share = (w * (1.0 / total)).astype(jnp.bfloat16)
            mixed = lax.dot_general(v, share, (((0,), (0,)), ((), ())), preferred_element_type=jnp.float32)
            mixed_ref[:, cols] = mixed.T.astype(jnp.bfloat16)
            lt_ref[h : h + 1, :] = top * SCALE + jnp.log(total)
    for d in range(send_ref.shape[0]):
        send_ref[d : d + 1, :] = lt_ref[pl.ds(head_of_ref[d], 1), :]


def slots_kernel(got_ref, slot_ref, out_ref):
    slots = slot_ref[...]
    row = slots >> 7
    lane = slots & 127
    out = jnp.zeros(slots.shape, jnp.float32)
    for r in range(got_ref.shape[0]):
        source = jnp.broadcast_to(got_ref[r : r + 1, :], slots.shape)
        out = jnp.where(row == r, jnp.take_along_axis(source, lane, axis=1), out)
    for r in range(slots.shape[0]):
        out_ref[:, r * 128 : (r + 1) * 128] = out[r : r + 1, :]


def streamed(tokens_ref, weight_ref, held_ref, rows_ref, sems):
    count = sems.shape[0] - 1
    step = weight_ref.shape[0] // count
    parts = [pl.ds(i * step, step) for i in range(count)]
    tokens = pltpu.make_async_copy(tokens_ref, rows_ref, sems.at[count])
    copies = [pltpu.make_async_copy(weight_ref.at[p], held_ref.at[p], sems.at[i]) for i, p in enumerate(parts)]
    tokens.start()
    for copy in copies:
        copy.start()
    tokens.wait()
    total = None
    for copy, part in zip(copies, parts):
        copy.wait()
        product = jnp.dot(rows_ref[:, part], held_ref[part, :], preferred_element_type=jnp.float32)
        total = product if total is None else total + product
    return total


def away_kernel(tokens_ref, weight_ref, out_ref, held_ref, rows_ref, sems):
    out_ref[...] = streamed(tokens_ref, weight_ref, held_ref, rows_ref, sems).astype(jnp.bfloat16)


def here_kernel(side_ref, tokens_ref, weight_ref, residual_ref, out_ref, held_ref, rows_ref, sems, half_ref, sem):
    width = half_ref.shape[1]
    mine = pl.ds(pl.multiple_of(side_ref[0] * width, width), width)
    total = streamed(tokens_ref, weight_ref, held_ref, rows_ref, sems)
    half_ref[...] = (residual_ref[:, mine].astype(jnp.float32) + total).astype(jnp.bfloat16)
    copy = pltpu.make_async_copy(half_ref, out_ref.at[:, mine], sem)
    copy.start()
    copy.wait()


def join_kernel(side_ref, here_ref, back_ref, residual_ref, out_ref, half_ref, sem):
    width = half_ref.shape[1]
    theirs = pl.ds(pl.multiple_of((1 - side_ref[0]) * width, width), width)
    total = residual_ref[:, theirs].astype(jnp.float32) + back_ref[...].astype(jnp.float32)
    half_ref[...] = total.astype(jnp.bfloat16)
    copy = pltpu.make_async_copy(half_ref, out_ref.at[:, theirs], sem)
    copy.start()
    copy.wait()


def fetch_kernel(source_ref, out_ref, sem):
    copy = pltpu.make_async_copy(source_ref, out_ref, sem)
    copy.start()
    copy.wait()


def after(x, *others):
    whole = pl.BlockSpec(memory_space=pltpu.VMEM)
    return pl.pallas_call(
        lambda *refs: None,
        out_shape=jax.ShapeDtypeStruct(x.shape, x.dtype),
        in_specs=[whole] * (1 + len(others)),
        out_specs=whole,
        input_output_aliases={0: 0},
        compiler_params=VMEM,
    )(x, *others)


def local(query, key_proj, value_projection_side, residual, w_out, doc_ids, slot_token, head_of):
    tok_rows = query.shape[1]
    heads = query.shape[2] // HEAD_SIZE
    kv_heads = key_proj.shape[2] // HEAD_SIZE
    seq_count = lax.axis_size(SEQ)
    me = lax.axis_index(SEQ)
    core = lax.axis_index("core")
    side = (lax.axis_index("x") + lax.axis_index("z")) % 2
    half = w_out.shape[0] // 2
    columns = w_out.shape[1]
    width = columns // 2
    swap = [(i, i ^ 1) for i in range(seq_count)]
    cores, row = lax.axis_size("core"), lax.axis_size("z") * lax.axis_size("core")
    pair = [(i, (i // row ^ 1) * row + i % row if i % cores == 0 else i ^ cores) for i in range(seq_count)]

    anywhere = pl.BlockSpec(memory_space=pl.ANY)
    whole = pl.BlockSpec(memory_space=pltpu.VMEM)
    scalars = pl.BlockSpec(memory_space=pltpu.SMEM)
    part = lax.dynamic_slice(w_out, (core * half, side * width), (half, width))
    weight = lax.all_gather(part, ("fsdp", "core"), axis=0, tiled=True)

    kv = jnp.concatenate([key_proj[0], value_projection_side[0]], axis=1)
    kv1 = lax.ppermute(kv, SEQ, [(i, (i + 2) % seq_count) for i in range(seq_count)])
    kv2 = lax.ppermute(kv, SEQ, [(i, (i + (3 if i % 2 else 1)) % seq_count) for i in range(seq_count)])
    queries = pl.pallas_call(
        fetch_kernel,
        out_shape=jax.ShapeDtypeStruct(query.shape[1:], query.dtype),
        in_specs=[pl.BlockSpec(memory_space=pl.ANY)],
        out_specs=pl.BlockSpec(memory_space=pltpu.VMEM),
        scratch_shapes=[pltpu.SemaphoreType.DMA],
        compiler_params=VMEM,
    )(query[0])
    kv1 = after(kv1, queries)
    kv3 = lax.ppermute(kv1, SEQ, swap)

    back_rows = BACK * tok_rows
    padded = jnp.concatenate([jnp.full((back_rows,), -1, jnp.int32), doc_ids[0]])
    behind = (0, 2, 3 - 2 * core, 1 + 2 * core)
    query_docs = lax.dynamic_slice_in_dim(padded, (me + BACK) * tok_rows, tok_rows, 0)
    docs = jnp.concatenate([lax.dynamic_slice_in_dim(padded, (me + BACK - b) * tok_rows, tok_rows, 0) for b in behind])
    key_at = jnp.arange((BACK + 1) * tok_rows, dtype=jnp.int32)
    query_at = jnp.arange(tok_rows, dtype=jnp.int32)
    allowed = (docs[:, None] == query_docs[None, :]) & (
        (key_at[:, None] >= tok_rows) | (key_at[:, None] <= query_at[None, :])
    )
    bias = jnp.where(allowed, 0.0, -1e30).astype(jnp.float32)

    mixed, send = pl.pallas_call(
        functools.partial(attend_kernel, heads, kv_heads),
        out_shape=(
            jax.ShapeDtypeStruct((tok_rows, heads * HEAD_SIZE), jnp.bfloat16),
            jax.ShapeDtypeStruct((seq_count, tok_rows), jnp.float32),
        ),
        in_specs=[scalars] + [whole] * 6,
        out_specs=(whole, whole),
        scratch_shapes=[pltpu.VMEM((heads, tok_rows), jnp.float32)],
        compiler_params=VMEM,
    )(head_of, queries, bias, kv, kv1, kv2, kv3)

    theirs = lax.ppermute(mixed, SEQ, pair)
    got = lax.all_to_all(send, SEQ, split_axis=0, concat_axis=0, tiled=True)
    capacity = slot_token.shape[1]
    stats = pl.pallas_call(
        slots_kernel,
        out_shape=jax.ShapeDtypeStruct((1, capacity), jnp.float32),
        in_specs=[whole, whole],
        out_specs=whole,
        compiler_params=VMEM,
    )(got, slot_token.reshape(capacity // 128, 128))
    theirs = after(theirs, stats)
    scratch = [
        pltpu.VMEM((columns, width), jnp.bfloat16),
        pltpu.VMEM((tok_rows, columns), jnp.bfloat16),
        pltpu.SemaphoreType.DMA((9,)),
    ]
    half_scratch = [pltpu.VMEM((tok_rows, width), jnp.bfloat16), pltpu.SemaphoreType.DMA]
    away = pl.pallas_call(
        away_kernel,
        out_shape=jax.ShapeDtypeStruct((tok_rows, width), jnp.bfloat16),
        in_specs=[anywhere, anywhere],
        out_specs=whole,
        scratch_shapes=scratch,
        compiler_params=STREAM,
    )(theirs, weight)
    back = lax.ppermute(away, SEQ, pair)
    result = jax.ShapeDtypeStruct((tok_rows, columns), jnp.bfloat16)
    side = side[None].astype(jnp.int32)
    here = pl.pallas_call(
        here_kernel,
        out_shape=result,
        in_specs=[scalars, anywhere, anywhere, whole],
        out_specs=anywhere,
        scratch_shapes=scratch + half_scratch,
        compiler_params=STREAM,
    )(side, mixed, weight, residual[0])
    layer_out = pl.pallas_call(
        join_kernel,
        out_shape=result,
        in_specs=[scalars, anywhere, whole, whole],
        out_specs=anywhere,
        scratch_shapes=half_scratch,
        input_output_aliases={1: 0},
        compiler_params=VMEM,
    )(side, here, back, residual[0])
    return (layer_out[None], stats)


def solution(mesh):
    split = Mesh(mesh.devices.reshape(4, 8, 2, 8), ("x", "z", "core", "fsdp"))
    return jax.shard_map(
        local,
        mesh=split,
        in_specs=(
            P("fsdp", SEQ, None),
            P("fsdp", SEQ, None),
            P("fsdp", SEQ, None),
            P("fsdp", SEQ, None),
            P("fsdp", None),
            P("fsdp", None),
            P("fsdp", SEQ),
            P(),
        ),
        out_specs=(P("fsdp", SEQ, None), P("fsdp", SEQ)),
        check_vma=False,
    )
```

```python
import functools
import math

import jax
import jax.numpy as jnp
from jax import lax
from jax.experimental import pallas as pl
from jax.experimental.pallas import tpu as pltpu
from jax.sharding import Mesh, PartitionSpec as P

HEAD_SIZE = 128
BLOCK = 128
BACK = 3
SCALE = 1.0 / math.sqrt(HEAD_SIZE)
SEQ = ("x", "z", "core")
VMEM = pltpu.CompilerParams(vmem_limit_bytes=14 * 1024 * 1024)


def attend_kernel(heads, kv_heads, head_of_ref, q_ref, bias_ref, kv0_ref, kv1_ref, kv2_ref, kv3_ref, mixed_ref, send_ref, lt_ref):
    per = heads // kv_heads
    width = kv_heads * HEAD_SIZE
    pieces = (kv0_ref, kv1_ref, kv2_ref, kv3_ref)
    bias = bias_ref[...]
    for g in range(kv_heads):
        at = g * HEAD_SIZE
        k = jnp.concatenate([p[:, at : at + HEAD_SIZE] for p in pieces], axis=0)
        v = jnp.concatenate([p[:, width + at : width + at + HEAD_SIZE] for p in pieces], axis=0)
        for h in range(g * per, (g + 1) * per):
            cols = slice(h * HEAD_SIZE, (h + 1) * HEAD_SIZE)
            s = lax.dot_general(k, q_ref[:, cols], (((1,), (1,)), ((), ())), preferred_element_type=jnp.float32)
            s = s + bias
            top = jnp.max(s, axis=0, keepdims=True)
            w = jnp.exp2((s - top) * (SCALE * math.log2(math.e)))
            total = jnp.sum(w, axis=0, keepdims=True)
            share = (w * (1.0 / total)).astype(jnp.bfloat16)
            mixed = lax.dot_general(v, share, (((0,), (0,)), ((), ())), preferred_element_type=jnp.float32)
            mixed_ref[:, cols] = mixed.T.astype(jnp.bfloat16)
            lt_ref[h : h + 1, :] = top * SCALE + jnp.log(total)
    for d in range(send_ref.shape[0]):
        send_ref[d : d + 1, :] = lt_ref[pl.ds(head_of_ref[d], 1), :]


def slots_kernel(got_ref, slot_ref, out_ref):
    slots = slot_ref[...]
    row = slots >> 7
    lane = slots & 127
    out = jnp.zeros(slots.shape, jnp.float32)
    for r in range(got_ref.shape[0]):
        source = jnp.broadcast_to(got_ref[r : r + 1, :], slots.shape)
        out = jnp.where(row == r, jnp.take_along_axis(source, lane, axis=1), out)
    for r in range(slots.shape[0]):
        out_ref[:, r * 128 : (r + 1) * 128] = out[r : r + 1, :]


def away_kernel(tokens_ref, weight_ref, out_ref):
    total = jnp.dot(tokens_ref[...], weight_ref[...], preferred_element_type=jnp.float32)
    out_ref[...] = total.astype(jnp.bfloat16)


def here_kernel(side_ref, tokens_ref, weight_ref, residual_ref, out_ref, half_ref, sem):
    width = half_ref.shape[1]
    mine = pl.ds(pl.multiple_of(side_ref[0] * width, width), width)
    total = jnp.dot(tokens_ref[...], weight_ref[...], preferred_element_type=jnp.float32)
    half_ref[...] = (residual_ref[:, mine].astype(jnp.float32) + total).astype(jnp.bfloat16)
    copy = pltpu.make_async_copy(half_ref, out_ref.at[:, mine], sem)
    copy.start()
    copy.wait()


def join_kernel(side_ref, here_ref, back_ref, residual_ref, out_ref, half_ref, sem):
    width = half_ref.shape[1]
    theirs = pl.ds(pl.multiple_of((1 - side_ref[0]) * width, width), width)
    total = residual_ref[:, theirs].astype(jnp.float32) + back_ref[...].astype(jnp.float32)
    half_ref[...] = total.astype(jnp.bfloat16)
    copy = pltpu.make_async_copy(half_ref, out_ref.at[:, theirs], sem)
    copy.start()
    copy.wait()


def fetch_kernel(source_ref, out_ref, sem):
    copy = pltpu.make_async_copy(source_ref, out_ref, sem)
    copy.start()
    copy.wait()


def after(x, *others):
    whole = pl.BlockSpec(memory_space=pltpu.VMEM)
    return pl.pallas_call(
        lambda *refs: None,
        out_shape=jax.ShapeDtypeStruct(x.shape, x.dtype),
        in_specs=[whole] * (1 + len(others)),
        out_specs=whole,
        input_output_aliases={0: 0},
        compiler_params=VMEM,
    )(x, *others)


def local(query, key_proj, value_projection_side, residual, w_out, doc_ids, slot_token, head_of):
    tok_rows = query.shape[1]
    heads = query.shape[2] // HEAD_SIZE
    kv_heads = key_proj.shape[2] // HEAD_SIZE
    seq_count = lax.axis_size(SEQ)
    me = lax.axis_index(SEQ)
    core = lax.axis_index("core")
    side = (lax.axis_index("x") + lax.axis_index("z")) % 2
    half = w_out.shape[0] // 2
    columns = w_out.shape[1]
    width = columns // 2
    swap = [(i, i ^ 1) for i in range(seq_count)]
    cores, row = lax.axis_size("core"), lax.axis_size("z") * lax.axis_size("core")
    pair = [(i, (i // row ^ 1) * row + i % row if i % cores == 0 else i ^ cores) for i in range(seq_count)]

    anywhere = pl.BlockSpec(memory_space=pl.ANY)
    whole = pl.BlockSpec(memory_space=pltpu.VMEM)
    scalars = pl.BlockSpec(memory_space=pltpu.SMEM)
    part = lax.dynamic_slice(w_out, (core * half, side * width), (half, width))
    weight = lax.all_gather(part, ("fsdp", "core"), axis=0, tiled=True)

    kv = jnp.concatenate([key_proj[0], value_projection_side[0]], axis=1)
    kv1 = lax.ppermute(kv, SEQ, [(i, (i + 2) % seq_count) for i in range(seq_count)])
    kv2 = lax.ppermute(kv, SEQ, [(i, (i + (3 if i % 2 else 1)) % seq_count) for i in range(seq_count)])
    queries = pl.pallas_call(
        fetch_kernel,
        out_shape=jax.ShapeDtypeStruct(query.shape[1:], query.dtype),
        in_specs=[pl.BlockSpec(memory_space=pl.ANY)],
        out_specs=pl.BlockSpec(memory_space=pltpu.VMEM),
        scratch_shapes=[pltpu.SemaphoreType.DMA],
        compiler_params=VMEM,
    )(query[0])
    kv1 = after(kv1, queries)
    kv3 = lax.ppermute(kv1, SEQ, swap)

    back_rows = BACK * tok_rows
    padded = jnp.concatenate([jnp.full((back_rows,), -1, jnp.int32), doc_ids[0]])
    behind = (0, 2, 3 - 2 * core, 1 + 2 * core)
    query_docs = lax.dynamic_slice_in_dim(padded, (me + BACK) * tok_rows, tok_rows, 0)
    docs = jnp.concatenate([lax.dynamic_slice_in_dim(padded, (me + BACK - b) * tok_rows, tok_rows, 0) for b in behind])
    key_at = jnp.arange((BACK + 1) * tok_rows, dtype=jnp.int32)
    query_at = jnp.arange(tok_rows, dtype=jnp.int32)
    allowed = (docs[:, None] == query_docs[None, :]) & (
        (key_at[:, None] >= tok_rows) | (key_at[:, None] <= query_at[None, :])
    )
    bias = jnp.where(allowed, 0.0, -1e30).astype(jnp.float32)

    mixed, send = pl.pallas_call(
        functools.partial(attend_kernel, heads, kv_heads),
        out_shape=(
            jax.ShapeDtypeStruct((tok_rows, heads * HEAD_SIZE), jnp.bfloat16),
            jax.ShapeDtypeStruct((seq_count, tok_rows), jnp.float32),
        ),
        in_specs=[scalars] + [whole] * 6,
        out_specs=(whole, whole),
        scratch_shapes=[pltpu.VMEM((heads, tok_rows), jnp.float32)],
        compiler_params=VMEM,
    )(head_of, queries, bias, kv, kv1, kv2, kv3)

    theirs = lax.ppermute(mixed, SEQ, pair)
    got = lax.all_to_all(send, SEQ, split_axis=0, concat_axis=0, tiled=True)
    capacity = slot_token.shape[1]
    stats = pl.pallas_call(
        slots_kernel,
        out_shape=jax.ShapeDtypeStruct((1, capacity), jnp.float32),
        in_specs=[whole, whole],
        out_specs=whole,
        compiler_params=VMEM,
    )(got, slot_token.reshape(capacity // 128, 128))
    theirs = after(theirs, stats)
    half_scratch = [pltpu.VMEM((tok_rows, width), jnp.bfloat16), pltpu.SemaphoreType.DMA]
    away = pl.pallas_call(
        away_kernel,
        out_shape=jax.ShapeDtypeStruct((tok_rows, width), jnp.bfloat16),
        in_specs=[whole, whole],
        out_specs=whole,
        compiler_params=VMEM,
    )(theirs, weight)
    back = lax.ppermute(away, SEQ, pair)
    result = jax.ShapeDtypeStruct((tok_rows, columns), jnp.bfloat16)
    side = side[None].astype(jnp.int32)
    here = pl.pallas_call(
        here_kernel,
        out_shape=result,
        in_specs=[scalars] + [whole] * 3,
        out_specs=anywhere,
        scratch_shapes=half_scratch,
        compiler_params=VMEM,
    )(side, mixed, weight, residual[0])
    layer_out = pl.pallas_call(
        join_kernel,
        out_shape=result,
        in_specs=[scalars, anywhere, whole, whole],
        out_specs=anywhere,
        scratch_shapes=half_scratch,
        input_output_aliases={1: 0},
        compiler_params=VMEM,
    )(side, here, back, residual[0])
    return (layer_out[None], stats)


def solution(mesh):
    split = Mesh(mesh.devices.reshape(4, 8, 2, 8), ("x", "z", "core", "fsdp"))
    return jax.shard_map(
        local,
        mesh=split,
        in_specs=(
            P("fsdp", SEQ, None),
            P("fsdp", SEQ, None),
            P("fsdp", SEQ, None),
            P("fsdp", SEQ, None),
            P("fsdp", None),
            P("fsdp", None),
            P("fsdp", SEQ),
            P(),
        ),
        out_specs=(P("fsdp", SEQ, None), P("fsdp", SEQ)),
        check_vma=False,
    )
```
